256 devices in a mesh: row: 32 (over z, y), col: 8 (over x, core).
Axes of the slice: x: 4, y: 4, z: 8, core: 2. Of those that a mesh axis runs over, the one named last changes fastest.
Arguments:
- inputs: bfloat16 [2048, 12288], P('row', 'col'), may hold values from -6 to 6
- preact: bfloat16 [2048, 24576], P('col', 'row'), may hold values from -8 to 8
- out_grad: bfloat16 [2048, 12288], P('row', 'col'), may hold values from -6 to 6
- w_in: bfloat16 [12288, 24576], P('col', 'row'), may hold values from -0.0546875 to 0.0546875
- w_out: bfloat16 [24576, 12288], P('row', 'col'), may hold values from -0.0390625 to 0.0390625
Outputs:
- input_grad: bfloat16 [2048, 12288], P('row', 'col')
- weight_grad: float32 [12288, 24576], P('col', 'row')
The draws below stay inside these ranges and needn't reach their ends.
All inputs are finite; a program needn't handle non-finite values.
Results may differ from the reference program's by a relative error of at most 0.005.
Values may be sent and summed in bfloat16 or wider, within the bound.
No kernel may reach another device: no remote copies, remote signals or barrier semaphores. Data moves between devices by JAX's collectives and lax.ppermute only.
A program may use at most 128 MiB of HBM per device.

```python
import jax
import jax.numpy as jnp
from jax import lax

D = 12288
FF = 24576
TOKENS = 2048


def steps_of(stream_key, extent, cuts, least, top_value):
    def one(axis_at, blocks):
        heights = jax.random.uniform(jax.random.fold_in(jax.random.fold_in(stream_key, 6), axis_at), (blocks,), jnp.float32, least / len(cuts), top_value / len(cuts))
        return jnp.repeat(jnp.exp(heights), extent[axis_at] // blocks).reshape((-1,) + (1,) * (len(extent) - axis_at - 1))

    loudness = one(*cuts[0])
    for cut in cuts[1:]:
        loudness = loudness * one(*cut)
    return loudness


def centred(rng, shape, scale, most, pieces=(), kind=jnp.bfloat16):
    level = steps_of(rng, shape, pieces, -0.22, 0.18) if pieces else 1.0
    entries = jax.random.normal(rng, shape, jnp.float32) * scale * level
    return jnp.minimum(jnp.maximum(entries, -most), most).astype(kind)


def setup_inputs(seed: int = 0) -> dict:
    key_of = jax.random.split(jax.random.key(seed), 6)
    return {
        "inputs": centred(key_of[0], (TOKENS, D), 1.0, 6.0, ((0, 32), (1, 8))),
        "preact": centred(key_of[1], (TOKENS, FF), 1.5, 8.0, ((0, 8), (1, 32))),
        "out_grad": centred(key_of[2], (TOKENS, D), 1.0, 6.0, ((0, 32), (1, 8))),
        "w_in": centred(key_of[3], (D, FF), D ** -0.5, 0.0546875, ((0, 8), (1, 32))),
        "w_out": centred(key_of[4], (FF, D), FF ** -0.5, 0.0390625, ((0, 32), (1, 8))),
    }


def gelu_slope(pre):
    value = pre.astype(jnp.float32)
    normal_cdf = 0.5 * (1.0 + jax.scipy.special.erf(value * 0.7071067811865476))
    density = jnp.exp(-0.5 * value * value) * 0.3989422804014327
    return normal_cdf + value * density


def reference(inputs, preact, out_grad, w_in, w_out):
    second = (((1,), (1,)), ((), ()))
    first = (((0,), (0,)), ((), ()))
    act_grad = lax.dot_general(out_grad, w_out, second, preferred_element_type=jnp.float32)
    hidden_grad = (act_grad * gelu_slope(preact)).astype(jnp.bfloat16)
    weight_grad = lax.dot_general(inputs, hidden_grad, first, preferred_element_type=jnp.float32)
    input_grad = lax.dot_general(hidden_grad, w_in, second, preferred_element_type=jnp.float32)
    return input_grad.astype(jnp.bfloat16), weight_grad
```

```python
import jax
import jax.numpy as jnp
from jax import lax
from jax.experimental import pallas as pl
from jax.experimental.pallas import tpu as pltpu
from jax.sharding import Mesh, PartitionSpec as P

Z, Y, X, C = 8, 4, 4, 2
SIZE = {"z": Z, "y": Y, "x": X, "core": C}
GROUPS = (((1, 0), True), ((2, 3), True), ((4, 5), True), ((6,), False), ((7,), False))
BF16, F32 = jnp.bfloat16, jnp.float32


def shift(a, axis, by):
    n = SIZE[axis]
    return lax.ppermute(a, axis, [(i, (i - by) % n) for i in range(n)])


def swap(a):
    return lax.ppermute(a, "core", [(0, 1), (1, 0)])


def ring(a, axis):
    n = SIZE[axis]
    pairs = [
        (C * i + c, C * ((i + (1 if c == 0 else -1)) % n) + c)
        for i in range(n)
        for c in range(C)
    ]
    return lax.ppermute(a, (axis, "core"), pairs)


def after(a, *others):
    return lax.optimization_barrier((a,) + others)[0] if others else a


def pick(a, i):
    return lax.dynamic_index_in_dim(a, i, 0, keepdims=False)


def gelu_slope(pre):
    value = pre.astype(F32)
    normal_cdf = 0.5 * (1.0 + lax.erf(value * 0.7071067811865476))
    density = jnp.exp(-0.5 * value * value) * 0.3989422804014327
    return normal_cdf + value * density


def weight_kernel(place, tokens_ref, *refs):
    parts, (out_ref, hidden) = refs[:-2], refs[-2:]
    half = len(parts) // 2

    @pl.when(pl.program_id(0) == 0)
    def _():
        z, y, x, core = place[0], place[1], place[2], place[3]
        for who in range(2):
            c = core if who == 0 else 1 - core
            sign = 1 - 2 * c
            for part, (js, _) in zip(parts[half * who : half * (who + 1)], GROUPS):
                for p in range(X):
                    row_y = lax.rem(y + lax.rem(x + p, X), Y)
                    for n, j in enumerate(js):
                        row_z = lax.rem(z - sign * j + 2 * Z, Z)
                        hidden[row_y * Z + row_z, c] = part[p, n]

    out_ref[...] = lax.dot_general(
        tokens_ref[...],
        hidden[...].reshape(tokens_ref.shape[0], -1),
        (((0,), (0,)), ((), ())),
        preferred_element_type=F32,
    )


def weight_product(place, tokens, parts):
    total, width = tokens.shape
    half, ff = parts[0].shape[-2:]
    block = 256
    return pl.pallas_call(
        weight_kernel,
        grid_spec=pltpu.PrefetchScalarGridSpec(
            num_scalar_prefetch=1,
            grid=(width // block,),
            in_specs=[pl.BlockSpec((total, block), lambda i, _: (0, i))]
            + [pl.BlockSpec(p.shape, lambda i, _: (0, 0, 0, 0)) for p in parts],
            out_specs=pl.BlockSpec((block, ff), lambda i, _: (i, 0)),
            scratch_shapes=[pltpu.VMEM((Z * Y, C, half, ff), BF16)],
        ),
        out_shape=jax.ShapeDtypeStruct((width, ff), F32),
        compiler_params=pltpu.CompilerParams(vmem_limit_bytes=40 * 2**20),
        cost_estimate=pl.CostEstimate(
            flops=2 * total * width * ff,
            bytes_accessed=2 * total * (width + ff) + 4 * width * ff,
            transcendentals=0,
        ),
        name="weight_product",
    )(place, tokens, *parts)


def per_device(inputs, preact, out_grad, w_in, w_out):
    z, y = lax.axis_index("z"), lax.axis_index("y")
    x, core = lax.axis_index("x"), lax.axis_index("core")
    second = (((1,), (1,)), ((), ()))
    width, ff = out_grad.shape[1], w_out.shape[0]
    both, half = 2 * width, out_grad.shape[0] // 2
    sign = 1 - 2 * core

    inputs_all = lax.all_gather(inputs, "z", axis=0, tiled=True)
    inputs_all = lax.all_gather(inputs_all, "y", axis=0, tiled=True)

    mine = lax.dynamic_slice_in_dim(out_grad, core * half, half, 0)
    theirs = lax.dynamic_slice_in_dim(out_grad, (1 - core) * half, half, 0)
    grads = jnp.concatenate([mine, swap(theirs)], axis=1)

    blocks = [jnp.stack([grads] + [shift(grads, "y", d) for d in range(1, Y)])]
    w_out2 = jnp.concatenate([w_out, swap(after(w_out, grads))], axis=1)
    w_in2 = jnp.concatenate([w_in, swap(after(w_in, grads))], axis=0)

    pre = preact.reshape(Y, 2, half, ff)
    near = after(lax.dynamic_index_in_dim(pre, core, 1, keepdims=False), grads)
    far = after(lax.dynamic_index_in_dim(pre, 1 - core, 1, keepdims=False), grads)
    pair = jnp.stack([near, swap(far)], axis=1)
    pre = jnp.stack(
        [pick(pair, (y + x) % Y)]
        + [shift(pick(pair, (y + x - d) % Y), "x", d) for d in range(1, X)]
    ).reshape(2 * X, half, ff)

    def pre_of(j):
        at = (z - sign * j) % Z
        d, other = (at // 2 - x) % X, (at + core) % 2
        return lax.dynamic_slice_in_dim(pre, 2 * d + other, 1, 0)

    def act_of(js):
        rows = jnp.stack([blocks[j] for j in js], axis=1)
        return lax.dot_general(
            rows.reshape(-1, both), w_out2, second, preferred_element_type=F32
        ).reshape(X, len(js), half, ff)

    def hidden_of(act, js, wide):
        total = pick(act, x)
        for d in range(1, X):
            part = pick(act, (x - d) % X)
            part = part if wide else part.astype(BF16)
            total = total + shift(part, "x", d).astype(F32)
        slope = gelu_slope(jnp.concatenate([pre_of(j) for j in js]))
        return (total * slope).astype(BF16)

    def everyones(hidden):
        return jnp.stack([hidden] + [shift(hidden, "x", d) for d in range(1, X)])

    def out_of(part):
        out = lax.dot_general(
            part.reshape(-1, ff), w_in2, second, preferred_element_type=F32
        )
        return out.reshape(part.shape[:3] + (both,))

    acts, hiddens, parts, outs, grads_of = [], [], [], [], {}
    def do(kind, g):
        js, wide = GROUPS[g]
        if kind == "act":
            acts.append(act_of(js))
            return acts[g]
        if kind == "hidden":
            hiddens.append(hidden_of(acts[g], js, wide))
            return hiddens[g]
        parts.append(everyones(hiddens[g]))
        outs.append(out_of(parts[g]))
        return outs[g]

    ahead = {
        3: [("act", 0), ("hidden", 0)],
        4: [("out", 0), ("act", 1)],
        5: [("hidden", 1)],
        6: [("out", 1), ("act", 2)],
        7: [("hidden", 2)],
    }
    for j in range(1, Z):
        others = [do(*what) for what in ahead.get(j, [])]
        others += [w_out2] if j == 1 else [w_in2, pre] if j == 2 else []
        blocks.append(ring(after(blocks[-1], *others), "z"))
    late = {4: [("out", 2), ("act", 3), ("hidden", 3)], 5: [("act", 4), ("hidden", 4)]}
    late |= {6: [("out", 3)], 7: [("out", 4)]}
    late = {j: [do(*what) for what in whats] for j, whats in late.items()}
    for (js, _), out in zip(GROUPS, outs):
        for n, j in enumerate(js):
            grads_of[j] = out[:, n]

    place = jnp.stack([z, y, x, core]).astype(jnp.int32)
    weight_grad = weight_product(
        place, inputs_all, parts + [swap(p) for p in parts]
    )

    grads_of[0] = after(grads_of[0], weight_grad)
    total = grads_of[1]
    for j in range(1, Z):
        part = after(total.astype(BF16), *late.get(j, []))
        total = ring(part, "z").astype(F32) + grads_of[(j + 1) % Z]
    own = pick(total, (0 - x) % X)
    for d in range(1, Y):
        own = own + shift(pick(total, (Y - d - x) % X).astype(BF16), "y", d).astype(F32)
    own = own.astype(BF16)
    kept, given = own[:, :width], swap(own[:, width:])
    input_grad = jnp.where(
        core == 0, jnp.concatenate([kept, given]), jnp.concatenate([given, kept])
    )

    return input_grad, weight_grad


def solution(mesh):
    grid = Mesh(mesh.devices.reshape(Z, Y, X, C), ("z", "y", "x", "core"))
    row, col = ("z", "y"), ("x", "core")
    in_specs = (P(row, col), P(col, row), P(row, col), P(col, row), P(row, col))
    out_specs = (P(row, col), P(col, row))
    return jax.shard_map(
        per_device, mesh=grid, in_specs=in_specs, out_specs=out_specs, check_vma=False
    )
```

```python
import jax
import jax.numpy as jnp
from jax import lax
from jax.experimental import pallas as pl
from jax.experimental.pallas import tpu as pltpu
from jax.sharding import Mesh, PartitionSpec as P

Z, Y, X, C = 8, 4, 4, 2
SIZE = {"z": Z, "y": Y, "x": X, "core": C}
GROUPS = (((1, 0), False), ((2, 3), True), ((4, 5), True), ((6, 7), False))
BF16, F32 = jnp.bfloat16, jnp.float32


def shift(a, axis, by):
    n = SIZE[axis]
    return lax.ppermute(a, axis, [(i, (i - by) % n) for i in range(n)])


def swap(a):
    return lax.ppermute(a, "core", [(0, 1), (1, 0)])


def ring(a, axis):
    n = SIZE[axis]
    pairs = [
        (C * i + c, C * ((i + (1 if c == 0 else -1)) % n) + c)
        for i in range(n)
        for c in range(C)
    ]
    return lax.ppermute(a, (axis, "core"), pairs)


def together(*values):
    return lax.optimization_barrier(values)


def pick(a, i):
    return lax.dynamic_index_in_dim(a, i, 0, keepdims=False)


def gelu_slope(pre):
    value = pre.astype(F32)
    normal_cdf = 0.5 * (1.0 + lax.erf(value * 0.7071067811865476))
    density = jnp.exp(-0.5 * value * value) * 0.3989422804014327
    return normal_cdf + value * density


def weight_kernel(place, tokens_ref, *refs):
    parts, (out_ref, hidden) = refs[:-2], refs[-2:]
    half = len(parts) // 2

    @pl.when(pl.program_id(0) == 0)
    def _():
        z, y, x, core = place[0], place[1], place[2], place[3]
        for who in range(2):
            c = core if who == 0 else 1 - core
            sign = 1 - 2 * c
            for part, (js, _) in zip(parts[half * who : half * (who + 1)], GROUPS):
                for p in range(X):
                    row_y = lax.rem(y + lax.rem(x + p, X), Y)
                    for n, j in enumerate(js):
                        row_z = lax.rem(z - sign * j + 2 * Z, Z)
                        hidden[row_y * Z + row_z, c] = part[p, n]

    out_ref[...] = lax.dot_general(
        tokens_ref[...],
        hidden[...].reshape(tokens_ref.shape[0], -1),
        (((0,), (0,)), ((), ())),
        preferred_element_type=F32,
    )


def weight_product(place, tokens, parts):
    total, width = tokens.shape
    half, ff = parts[0].shape[-2:]
    block = 256
    return pl.pallas_call(
        weight_kernel,
        grid_spec=pltpu.PrefetchScalarGridSpec(
            num_scalar_prefetch=1,
            grid=(width // block,),
            in_specs=[pl.BlockSpec((total, block), lambda i, _: (0, i))]
            + [pl.BlockSpec(p.shape, lambda i, _: (0, 0, 0, 0)) for p in parts],
            out_specs=pl.BlockSpec((block, ff), lambda i, _: (i, 0)),
            scratch_shapes=[pltpu.VMEM((Z * Y, C, half, ff), BF16)],
        ),
        out_shape=jax.ShapeDtypeStruct((width, ff), F32),
        compiler_params=pltpu.CompilerParams(vmem_limit_bytes=20 * 2**20),
        cost_estimate=pl.CostEstimate(
            flops=2 * total * width * ff,
            bytes_accessed=2 * total * (width + ff) + 4 * width * ff,
            transcendentals=0,
        ),
        name="weight_product",
    )(place, tokens, *parts)


def per_device(inputs, preact, out_grad, w_in, w_out):
    z, y = lax.axis_index("z"), lax.axis_index("y")
    x, core = lax.axis_index("x"), lax.axis_index("core")
    second = (((1,), (1,)), ((), ()))
    width, ff = out_grad.shape[1], w_out.shape[0]
    both, half = 2 * width, out_grad.shape[0] // 2
    sign = 1 - 2 * core

    mine = lax.dynamic_slice_in_dim(out_grad, core * half, half, 0)
    theirs = lax.dynamic_slice_in_dim(out_grad, (1 - core) * half, half, 0)
    grads = jnp.concatenate([mine, swap(theirs)], axis=1)

    grads, inputs, w_out, w_in, preact = together(grads, inputs, w_out, w_in, preact)
    tokens = lax.all_gather(inputs, "z", axis=0, tiled=True)
    (w_out2,) = together(jnp.concatenate([w_out, swap(w_out)], axis=1))
    (w_in2,) = together(jnp.concatenate([w_in, swap(w_in)], axis=0))

    first = jnp.stack([grads] + [shift(grads, "y", d) for d in range(1, Y)])

    pre = preact.reshape(Y, 2, half, ff)
    near = lax.dynamic_index_in_dim(pre, core, 1, keepdims=False)
    far = lax.dynamic_index_in_dim(pre, 1 - core, 1, keepdims=False)
    pair = jnp.stack([near, swap(far)], axis=1)
    first, pair = together(first, pair)
    pre = jnp.stack(
        [pick(pair, (y + x) % Y)]
        + [shift(pick(pair, (y + x - d) % Y), "x", d) for d in range(1, X)]
    ).reshape(2 * X, half, ff)

    def pre_of(j):
        at = (z - sign * j) % Z
        d, other = (at // 2 - x) % X, (at + core) % 2
        return lax.dynamic_slice_in_dim(pre, 2 * d + other, 1, 0)

    def act_of(*got):
        return lax.dot_general(
            jnp.stack(got, axis=1).reshape(-1, both),
            w_out2,
            second,
            preferred_element_type=F32,
        ).reshape(X, len(got), half, ff)

    def terms_of(wide, act):
        terms = [pick(act, x)]
        for d in range(1, X):
            part = pick(act, (x - d) % X)
            terms.append(shift(part if wide else part.astype(BF16), "x", d))
        return terms

    def everyones(js, terms):
        slope = gelu_slope(jnp.concatenate([pre_of(j) for j in js]))
        hidden = (sum(t.astype(F32) for t in terms) * slope).astype(BF16)
        return jnp.stack([hidden] + [shift(hidden, "x", d) for d in range(1, X)])

    def out_of(part, n):
        return lax.dot_general(
            part[:, n].reshape(-1, ff), w_in2, second, preferred_element_type=F32
        ).reshape(X, half, both)

    def step_of(block):
        return ring(block, "z")

    def send(total, out):
        return ring((total.astype(F32) + out).astype(BF16), "z")

    (js0, wide0), (js1, wide1), (js2, wide2), (js3, wide3) = GROUPS
    step = step_of(first)
    act = act_of(step, first)
    step, act, pre = together(step, act, pre)

    last = step
    step, w_in2, tokens, *terms = together(
        step_of(step), w_in2, tokens, *terms_of(wide0, act)
    )
    part0 = everyones(js0, terms)
    last, step = step, step_of(step)
    act = act_of(last, step)
    step, act, part0 = together(step, act, part0)
    tokens = lax.all_gather(tokens, "y", axis=0, tiled=True)

    total = ring(out_of(part0, 0).astype(BF16), "z")
    zero = out_of(part0, 1)
    step, total, zero, *terms = together(
        step_of(step), total, zero, *terms_of(wide1, act)
    )
    part1 = everyones(js1, terms)
    last, step = step, step_of(step)
    act = act_of(last, step)
    step, act, part1, total = together(step, act, part1, total)

    total = send(total, out_of(part1, 0))
    three = out_of(part1, 1)
    step, total, three, *terms = together(
        step_of(step), total, three, *terms_of(wide2, act)
    )
    part2 = everyones(js2, terms)
    total = send(total, three)
    last, step = step, step_of(step)
    act = act_of(last, step)
    act, part2, total = together(act, part2, total)

    total = send(total, out_of(part2, 0))
    five = out_of(part2, 1)
    total, five, *terms = together(total, five, *terms_of(wide3, act))
    part3 = everyones(js3, terms)
    total = send(total, five)
    total, part3, six, tokens = together(total, part3, out_of(part3, 0), tokens)

    parts = [part0, part1, part2, part3]
    total = send(total, six)
    seven = out_of(part3, 1)
    total, seven, *others = together(total, seven, *[swap(p) for p in parts])
    total = send(total, seven)
    place = jnp.stack([z, y, x, core]).astype(jnp.int32)
    weight_grad = weight_product(place, tokens, parts + others)
    total, zero, weight_grad = together(total, zero, weight_grad)

    total = total.astype(F32) + zero
    own = pick(total, (0 - x) % X)
    for d in range(1, Y):
        own = own + shift(pick(total, (Y - d - x) % X).astype(BF16), "y", d).astype(F32)
    own = own.astype(BF16)
    kept, given = own[:, :width], swap(own[:, width:])
    input_grad = jnp.where(
        core == 0, jnp.concatenate([kept, given]), jnp.concatenate([given, kept])
    )

    return input_grad, weight_grad


def solution(mesh):
    grid = Mesh(mesh.devices.reshape(Z, Y, X, C), ("z", "y", "x", "core"))
    row, col = ("z", "y"), ("x", "core")
    in_specs = (P(row, col), P(col, row), P(row, col), P(col, row), P(row, col))
    out_specs = (P(row, col), P(col, row))
    return jax.shard_map(
        per_device, mesh=grid, in_specs=in_specs, out_specs=out_specs, check_vma=False
    )
```

```python
import jax
import jax.numpy as jnp
from jax import lax
from jax.experimental import pallas as pl
from jax.experimental.pallas import tpu as pltpu
from jax.sharding import Mesh, PartitionSpec as P

Z, Y, X, C = 8, 4, 4, 2
SIZE = {"z": Z, "y": Y, "x": X, "core": C}
GROUPS = (((1, 0), False), ((2, 3), True), ((4, 5), True), ((6, 7), False))
BF16, F32 = jnp.bfloat16, jnp.float32


def shift(a, axis, by):
    n = SIZE[axis]
    return lax.ppermute(a, axis, [(i, (i - by) % n) for i in range(n)])


def swap(a):
    return lax.ppermute(a, "core", [(0, 1), (1, 0)])


def ring(a, axis):
    n = SIZE[axis]
    pairs = [
        (C * i + c, C * ((i + (1 if c == 0 else -1)) % n) + c)
        for i in range(n)
        for c in range(C)
    ]
    return lax.ppermute(a, (axis, "core"), pairs)


def together(*values):
    return lax.optimization_barrier(values)


def pick(a, i):
    return lax.dynamic_index_in_dim(a, i, 0, keepdims=False)


def gelu_slope(pre):
    value = pre.astype(F32)
    normal_cdf = 0.5 * (1.0 + lax.erf(value * 0.7071067811865476))
    density = jnp.exp(-0.5 * value * value) * 0.3989422804014327
    return normal_cdf + value * density


def weight_kernel(place, tokens_ref, *refs):
    parts, (out_ref, hidden) = refs[:-2], refs[-2:]
    half = len(parts) // 2

    @pl.when(pl.program_id(0) == 0)
    def _():
        z, y, x, core = place[0], place[1], place[2], place[3]
        for who in range(2):
            c = core if who == 0 else 1 - core
            sign = 1 - 2 * c
            for part, (js, _) in zip(parts[half * who : half * (who + 1)], GROUPS):
                for p in range(X):
                    row_y = lax.rem(y + lax.rem(x + p, X), Y)
                    for n, j in enumerate(js):
                        row_z = lax.rem(z - sign * j + 2 * Z, Z)
                        hidden[row_y * Z + row_z, c] = part[p, n]

    out_ref[...] = lax.dot_general(
        tokens_ref[...],
        hidden[...].reshape(tokens_ref.shape[0], -1),
        (((0,), (0,)), ((), ())),
        preferred_element_type=F32,
    )


def weight_product(place, tokens, parts):
    total, width = tokens.shape
    half, ff = parts[0].shape[-2:]
    block = 256
    return pl.pallas_call(
        weight_kernel,
        grid_spec=pltpu.PrefetchScalarGridSpec(
            num_scalar_prefetch=1,
            grid=(width // block,),
            in_specs=[pl.BlockSpec((total, block), lambda i, _: (0, i))]
            + [pl.BlockSpec(p.shape, lambda i, _: (0, 0, 0, 0)) for p in parts],
            out_specs=pl.BlockSpec((block, ff), lambda i, _: (i, 0)),
            scratch_shapes=[pltpu.VMEM((Z * Y, C, half, ff), BF16)],
        ),
        out_shape=jax.ShapeDtypeStruct((width, ff), F32),
        compiler_params=pltpu.CompilerParams(vmem_limit_bytes=20 * 2**20),
        cost_estimate=pl.CostEstimate(
            flops=2 * total * width * ff,
            bytes_accessed=2 * total * (width + ff) + 4 * width * ff,
            transcendentals=0,
        ),
        name="weight_product",
    )(place, tokens, *parts)


def per_device(inputs, preact, out_grad, w_in, w_out):
    z, y = lax.axis_index("z"), lax.axis_index("y")
    x, core = lax.axis_index("x"), lax.axis_index("core")
    second = (((1,), (1,)), ((), ()))
    width, ff = out_grad.shape[1], w_out.shape[0]
    both, half = 2 * width, out_grad.shape[0] // 2
    sign = 1 - 2 * core

    mine = lax.dynamic_slice_in_dim(out_grad, core * half, half, 0)
    theirs = lax.dynamic_slice_in_dim(out_grad, (1 - core) * half, half, 0)
    grads = jnp.concatenate([mine, swap(theirs)], axis=1)

    grads, inputs, w_out, w_in, preact = together(grads, inputs, w_out, w_in, preact)
    tokens = lax.all_gather(inputs, "z", axis=0, tiled=True)
    (w_out2,) = together(jnp.concatenate([w_out, swap(w_out)], axis=1))
    (w_in2,) = together(jnp.concatenate([w_in, swap(w_in)], axis=0))

    first = jnp.stack([grads] + [shift(grads, "y", d) for d in range(1, Y)])

    pre = preact.reshape(Y, 2, half, ff)
    near = lax.dynamic_index_in_dim(pre, core, 1, keepdims=False)
    far = lax.dynamic_index_in_dim(pre, 1 - core, 1, keepdims=False)
    pair = jnp.stack([near, swap(far)], axis=1)
    first, pair = together(first, pair)
    pre = jnp.stack(
        [pick(pair, (y + x) % Y)]
        + [shift(pick(pair, (y + x - d) % Y), "x", d) for d in range(1, X)]
    ).reshape(2 * X, half, ff)

    def pre_of(j):
        at = (z - sign * j) % Z
        d, other = (at // 2 - x) % X, (at + core) % 2
        return lax.dynamic_slice_in_dim(pre, 2 * d + other, 1, 0)

    def act_of(*got):
        return lax.dot_general(
            jnp.stack(got, axis=1).reshape(-1, both),
            w_out2,
            second,
            preferred_element_type=F32,
        ).reshape(X, len(got), half, ff)

    def terms_of(wide, act):
        terms = [pick(act, x)]
        for d in range(1, X):
            part = pick(act, (x - d) % X)
            terms.append(shift(part if wide else part.astype(BF16), "x", d))
        return terms

    def everyones(js, terms):
        slope = gelu_slope(jnp.concatenate([pre_of(j) for j in js]))
        hidden = (sum(t.astype(F32) for t in terms) * slope).astype(BF16)
        return jnp.stack([hidden] + [shift(hidden, "x", d) for d in range(1, X)])

    def out_of(part, n):
        return lax.dot_general(
            part[:, n].reshape(-1, ff), w_in2, second, preferred_element_type=F32
        ).reshape(X, half, both)

    def step_of(block):
        return ring(block, "z")

    def send(total, out):
        return ring((total.astype(F32) + out).astype(BF16), "z")

    (js0, wide0), (js1, wide1), (js2, wide2), (js3, wide3) = GROUPS
    step, pre = together(step_of(first), pre)

    step, w_in2, *terms = together(
        step_of(step), w_in2, *terms_of(wide0, act_of(step, first))
    )
    part0 = everyones(js0, terms)
    last = step
    step, part0, tokens = together(step_of(step), part0, tokens)
    tokens = lax.all_gather(tokens, "y", axis=0, tiled=True)

    total = ring(out_of(part0, 0).astype(BF16), "z")
    zero = out_of(part0, 1)
    step, total, zero, *terms = together(
        step_of(step), total, zero, *terms_of(wide1, act_of(last, step))
    )
    part1 = everyones(js1, terms)
    last = step
    step, part1, total = together(step_of(step), part1, total)

    total = send(total, out_of(part1, 0))
    three = out_of(part1, 1)
    step, total, three, *terms = together(
        step_of(step), total, three, *terms_of(wide2, act_of(last, step))
    )
    part2 = everyones(js2, terms)
    total = send(total, three)
    last, step = step, step_of(step)
    act = act_of(last, step)
    act, part2, total = together(act, part2, total)

    total = send(total, out_of(part2, 0))
    five = out_of(part2, 1)
    total, five, *terms = together(total, five, *terms_of(wide3, act))
    part3 = everyones(js3, terms)
    total = send(total, five)
    total, part3, six, tokens = together(total, part3, out_of(part3, 0), tokens)

    parts = [part0, part1, part2, part3]
    total = send(total, six)
    seven = out_of(part3, 1)
    total, seven, *others = together(total, seven, *[swap(p) for p in parts])
    total = send(total, seven)
    place = jnp.stack([z, y, x, core]).astype(jnp.int32)
    weight_grad = weight_product(place, tokens, parts + others)
    total, zero, weight_grad = together(total, zero, weight_grad)

    total = total.astype(F32) + zero
    own = pick(total, (0 - x) % X)
    for d in range(1, Y):
        own = own + shift(pick(total, (Y - d - x) % X).astype(BF16), "y", d).astype(F32)
    own = own.astype(BF16)
    kept, given = own[:, :width], swap(own[:, width:])
    input_grad = jnp.where(
        core == 0, jnp.concatenate([kept, given]), jnp.concatenate([given, kept])
    )

    return input_grad, weight_grad


def solution(mesh):
    grid = Mesh(mesh.devices.reshape(Z, Y, X, C), ("z", "y", "x", "core"))
    row, col = ("z", "y"), ("x", "core")
    in_specs = (P(row, col), P(col, row), P(row, col), P(col, row), P(row, col))
    out_specs = (P(row, col), P(col, row))
    return jax.shard_map(
        per_device, mesh=grid, in_specs=in_specs, out_specs=out_specs, check_vma=False
    )
```

```python
import jax
import jax.numpy as jnp
from jax import lax
from jax.experimental import pallas as pl
from jax.experimental.pallas import tpu as pltpu
from jax.sharding import Mesh, PartitionSpec as P

Z, Y, X, C = 8, 4, 4, 2
SIZE = {"z": Z, "y": Y, "x": X, "core": C}
GROUPS = (((1, 0), False), ((2, 3), True), ((4, 5), True), ((6, 7), False))
BF16, F32 = jnp.bfloat16, jnp.float32


def shift(a, axis, by):
    n = SIZE[axis]
    return lax.ppermute(a, axis, [(i, (i - by) % n) for i in range(n)])


def swap(a):
    return lax.ppermute(a, "core", [(0, 1), (1, 0)])


def ring(a, axis):
    n = SIZE[axis]
    pairs = [
        (C * i + c, C * ((i + (1 if c == 0 else -1)) % n) + c)
        for i in range(n)
        for c in range(C)
    ]
    return lax.ppermute(a, (axis, "core"), pairs)


def together(*values):
    return lax.optimization_barrier(values)


def pick(a, i):
    return lax.dynamic_index_in_dim(a, i, 0, keepdims=False)


def gelu_slope(pre):
    value = pre.astype(F32)
    normal_cdf = 0.5 * (1.0 + lax.erf(value * 0.7071067811865476))
    density = jnp.exp(-0.5 * value * value) * 0.3989422804014327
    return normal_cdf + value * density


def weight_kernel(place, tokens_ref, *refs):
    parts, (out_ref, hidden) = refs[:-2], refs[-2:]
    half = len(parts) // 2

    @pl.when(pl.program_id(0) == 0)
    def _():
        z, y, x, core = place[0], place[1], place[2], place[3]
        for who in range(2):
            c = core if who == 0 else 1 - core
            sign = 1 - 2 * c
            for part, (js, _) in zip(parts[half * who : half * (who + 1)], GROUPS):
                for p in range(X):
                    row_y = lax.rem(y + lax.rem(x + p, X), Y)
                    for n, j in enumerate(js):
                        row_z = lax.rem(z - sign * j + 2 * Z, Z)
                        hidden[row_y * Z + row_z, c] = part[p, n]

    out_ref[...] = lax.dot_general(
        tokens_ref[...],
        hidden[...].reshape(tokens_ref.shape[0], -1),
        (((0,), (0,)), ((), ())),
        preferred_element_type=F32,
    )


def weight_product(place, tokens, parts):
    total, width = tokens.shape
    half, ff = parts[0].shape[-2:]
    block = 256
    return pl.pallas_call(
        weight_kernel,
        grid_spec=pltpu.PrefetchScalarGridSpec(
            num_scalar_prefetch=1,
            grid=(width // block,),
            in_specs=[pl.BlockSpec((total, block), lambda i, _: (0, i))]
            + [pl.BlockSpec(p.shape, lambda i, _: (0, 0, 0, 0)) for p in parts],
            out_specs=pl.BlockSpec((block, ff), lambda i, _: (i, 0)),
            scratch_shapes=[pltpu.VMEM((Z * Y, C, half, ff), BF16)],
        ),
        out_shape=jax.ShapeDtypeStruct((width, ff), F32),
        compiler_params=pltpu.CompilerParams(vmem_limit_bytes=20 * 2**20),
        cost_estimate=pl.CostEstimate(
            flops=2 * total * width * ff,
            bytes_accessed=2 * total * (width + ff) + 4 * width * ff,
            transcendentals=0,
        ),
        name="weight_product",
    )(place, tokens, *parts)


def per_device(inputs, preact, out_grad, w_in, w_out):
    z, y = lax.axis_index("z"), lax.axis_index("y")
    x, core = lax.axis_index("x"), lax.axis_index("core")
    second = (((1,), (1,)), ((), ()))
    width, ff = out_grad.shape[1], w_out.shape[0]
    both, half = 2 * width, out_grad.shape[0] // 2
    sign = 1 - 2 * core

    mine = lax.dynamic_slice_in_dim(out_grad, core * half, half, 0)
    theirs = lax.dynamic_slice_in_dim(out_grad, (1 - core) * half, half, 0)
    grads = jnp.concatenate([mine, swap(theirs)], axis=1)

    grads, inputs = together(grads, inputs)
    tokens = lax.all_gather(inputs, "z", axis=0, tiled=True)

    first = jnp.stack([grads] + [shift(grads, "y", d) for d in range(1, Y)])
    first, w_out, w_in, preact = together(first, w_out, w_in, preact)
    (w_out2,) = together(jnp.concatenate([w_out, swap(w_out)], axis=1))
    (w_in2,) = together(jnp.concatenate([w_in, swap(w_in)], axis=0))

    pre = preact.reshape(Y, 2, half, ff)
    near = lax.dynamic_index_in_dim(pre, core, 1, keepdims=False)
    far = lax.dynamic_index_in_dim(pre, 1 - core, 1, keepdims=False)
    pair = jnp.stack([near, swap(far)], axis=1)

    def pre_of(j):
        at = (z - sign * j) % Z
        d, other = (at // 2 - x) % X, (at + core) % 2
        return lax.dynamic_slice_in_dim(pre, 2 * d + other, 1, 0)

    def act_of(*got):
        return lax.dot_general(
            jnp.stack(got, axis=1).reshape(-1, both),
            w_out2,
            second,
            preferred_element_type=F32,
        ).reshape(X, len(got), half, ff)

    def terms_of(wide, act):
        terms = [pick(act, x)]
        for d in range(1, X):
            part = pick(act, (x - d) % X)
            terms.append(shift(part if wide else part.astype(BF16), "x", d))
        return terms

    def everyones(js, terms):
        slope = gelu_slope(jnp.concatenate([pre_of(j) for j in js]))
        hidden = (sum(t.astype(F32) for t in terms) * slope).astype(BF16)
        return jnp.stack([hidden] + [shift(hidden, "x", d) for d in range(1, X)])

    def out_of(part, n):
        return lax.dot_general(
            part[:, n].reshape(-1, ff), w_in2, second, preferred_element_type=F32
        ).reshape(X, half, both)

    def step_of(block):
        return ring(block, "z")

    def send(total, out):
        return ring((total.astype(F32) + out).astype(BF16), "z")

    (js0, wide0), (js1, wide1), (js2, wide2), (js3, wide3) = GROUPS
    step, pair = together(step_of(first), pair)
    pre = jnp.stack(
        [pick(pair, (y + x) % Y)]
        + [shift(pick(pair, (y + x - d) % Y), "x", d) for d in range(1, X)]
    ).reshape(2 * X, half, ff)

    step, w_in2, pre, *terms = together(
        step_of(step), w_in2, pre, *terms_of(wide0, act_of(step, first))
    )
    part0 = everyones(js0, terms)
    last = step
    step, part0, tokens = together(step_of(step), part0, tokens)
    tokens = lax.all_gather(tokens, "y", axis=0, tiled=True)

    total = ring(out_of(part0, 0).astype(BF16), "z")
    zero = out_of(part0, 1)
    step, total, zero, *terms = together(
        step_of(step), total, zero, *terms_of(wide1, act_of(last, step))
    )
    part1 = everyones(js1, terms)
    last = step
    step, part1, total = together(step_of(step), part1, total)

    total = send(total, out_of(part1, 0))
    three = out_of(part1, 1)
    step, total, three, *terms = together(
        step_of(step), total, three, *terms_of(wide2, act_of(last, step))
    )
    part2 = everyones(js2, terms)
    total = send(total, three)
    last, step = step, step_of(step)
    act = act_of(last, step)
    act, part2, total = together(act, part2, total)

    total = send(total, out_of(part2, 0))
    five = out_of(part2, 1)
    total, five, *terms = together(total, five, *terms_of(wide3, act))
    part3 = everyones(js3, terms)
    total = send(total, five)
    total, part3, six, tokens = together(total, part3, out_of(part3, 0), tokens)

    parts = [part0, part1, part2, part3]
    total = send(total, six)
    seven = out_of(part3, 1)
    total, seven, *others = together(total, seven, *[swap(p) for p in parts])
    total = send(total, seven)
    place = jnp.stack([z, y, x, core]).astype(jnp.int32)
    weight_grad = weight_product(place, tokens, parts + others)
    total, zero, weight_grad = together(total, zero, weight_grad)

    total = total.astype(F32) + zero
    own = pick(total, (0 - x) % X)
    for d in range(1, Y):
        own = own + shift(pick(total, (Y - d - x) % X).astype(BF16), "y", d).astype(F32)
    own = own.astype(BF16)
    kept, given = own[:, :width], swap(own[:, width:])
    input_grad = jnp.where(
        core == 0, jnp.concatenate([kept, given]), jnp.concatenate([given, kept])
    )

    return input_grad, weight_grad


def solution(mesh):
    grid = Mesh(mesh.devices.reshape(Z, Y, X, C), ("z", "y", "x", "core"))
    row, col = ("z", "y"), ("x", "core")
    in_specs = (P(row, col), P(col, row), P(row, col), P(col, row), P(row, col))
    out_specs = (P(row, col), P(col, row))
    return jax.shard_map(
        per_device, mesh=grid, in_specs=in_specs, out_specs=out_specs, check_vma=False
    )
```
